32 devices in a mesh: gx: 8 (over y, x, core), gy: 4 (over z).
Axes of the slice: x: 2, y: 2, z: 4, core: 2. Of those that a mesh axis runs over, the one named last changes fastest.
Arguments:
- theta: float32 [60, 256, 2048], P(None, 'gx', 'gy'), may hold values from -6 to 6
- winds: float32 [2, 60, 256, 2048], P(None, None, 'gx', 'gy'), may hold values from -4 to 4
- theta_bar: float32 [60, 256, 2048], P(None, 'gx', 'gy'), may hold values from -6 to 6
- press_bar: float32 [60, 256, 2048], P(None, 'gx', 'gy'), may hold values from -6 to 6
- urban_frac: float32 [256, 2048], P('gx', 'gy'), may hold values from 0.1 to 0.9
- wall_temp: float32 [256, 2048], P('gx', 'gy'), may hold values from -6 to 6
- urban_class: int32 [256, 2048], P('gx', 'gy'), may hold values from 0 to 10
- canopy_layers: int32 [256, 2048], P('gx', 'gy'), may hold values from 1 to 8
- height_bin: int32 [256, 2048], P('gx', 'gy'), may hold values from 0 to 14
- class_drag: float32 [11], replicated, may hold values from 0.05 to 0.5
- bin_profile: float32 [15, 60], replicated, may hold values from 0.2 to 1
- sound_coef: float32 [60], replicated, may hold values from 0.2 to 2
Outputs:
- theta_grad: float32 [60, 256, 2048], P(None, 'gx', 'gy')
- press_grad: float32 [60, 256, 2048], P(None, 'gx', 'gy')
- frac_grad: float32 [256, 2048], P('gx', 'gy')
- wall_grad: float32 [256, 2048], P('gx', 'gy')
The draws below stay inside these ranges and needn't reach their ends.
All inputs are finite; a program needn't handle non-finite values.
Results may differ from the reference program's by a relative error of at most 0.00016.
Values sent between devices are 32-bit elements; how exact they have to be, the bound alone decides.
A program may use at most 256 MiB of HBM per device.

```python
import math
import jax
import jax.numpy as jnp
from jax import lax

NZ = 60
NCLASS = 11
NBIN = 15
NLMAX = 8
NX = 256
NY = 2048


def with_ends(drawn, own_key, smallest, largest):
    longest = drawn.shape.index(max(drawn.shape))
    spots = []
    for shift in (0, 1):
        where = [jax.random.randint(jax.random.fold_in(own_key, axis), (), 0, length) for axis, length in enumerate(drawn.shape)]
        where[longest] = (where[longest] + shift) % drawn.shape[longest]
        spots.append(tuple(where))
    return drawn.at[spots[0]].set(smallest).at[spots[1]].set(largest)


def block_scale(key, dims, pieces, smallest, largest):
    factor_of = 1.0
    for dim, blocks in pieces:
        steps = jax.random.uniform(jax.random.fold_in(jax.random.fold_in(key, 6), dim), (blocks,), jnp.float32, smallest / len(pieces), largest / len(pieces))
        factor_of = factor_of * jnp.repeat(jnp.exp(steps), dims[dim] // blocks).reshape((-1,) + (1,) * (len(dims) - 1 - dim))
    return factor_of


def centred(stream_key, extent, scale, most, split=(), kind=jnp.bfloat16):
    level = block_scale(stream_key, extent, split, -0.22, 0.18) if split else 1.0
    values = jax.random.normal(stream_key, extent, jnp.float32) * scale * level
    return jnp.minimum(jnp.maximum(values, -most), most).astype(kind)


def setup_inputs(seed: int = 0) -> dict:
    key_list = jax.random.split(jax.random.key(seed), 13)
    return {
        "theta": centred(key_list[0], (NZ, NX, NY), 1.0, 6.0, ((1, 8), (2, 4)), jnp.float32),
        "winds": centred(key_list[1], (2, NZ, NX, NY), 1.0, 4.0, ((2, 8), (3, 4)), jnp.float32),
        "theta_bar": centred(key_list[2], (NZ, NX, NY), 1.0, 6.0, ((1, 8), (2, 4)), jnp.float32),
        "press_bar": centred(key_list[3], (NZ, NX, NY), 1.0, 6.0, ((1, 8), (2, 4)), jnp.float32),
        "urban_frac": jnp.clip(0.1 + 0.79999997 * jax.random.uniform(key_list[4], (NX, NY), jnp.float32) ** block_scale(key_list[4], (NX, NY), ((0, 8), (1, 4)), -0.2, 0.2), 0.1, 0.9),
        "wall_temp": centred(key_list[5], (NX, NY), 1.0, 6.0, ((0, 8), (1, 4)), jnp.float32),
        "urban_class": with_ends(jax.random.randint(key_list[6], (NX, NY), 0, NCLASS), jax.random.fold_in(key_list[6], 1), 0, NCLASS - 1).astype(jnp.int32),
        "canopy_layers": with_ends(jax.random.randint(key_list[7], (NX, NY), 1, NLMAX + 1), jax.random.fold_in(key_list[7], 1), 1, NLMAX).astype(jnp.int32),
        "height_bin": with_ends(jax.random.randint(key_list[8], (NX, NY), 0, NBIN), jax.random.fold_in(key_list[8], 1), 0, NBIN - 1).astype(jnp.int32),
        "class_drag": jnp.clip(jnp.exp(jax.random.uniform(key_list[9], (NCLASS,), jnp.float32, math.log(0.05), math.log(0.5))), 0.05, 0.5),
        "bin_profile": jnp.clip(jax.random.uniform(key_list[10], (NBIN, NZ), jnp.float32, 0.2, 1.0), 0.2, 1.0),
        "sound_coef": jnp.clip(jnp.exp(jax.random.uniform(key_list[11], (NZ,), jnp.float32, math.log(0.2), math.log(2.0))), 0.2, 2.0),
    }


courant = 0.3
diffusion = 0.1
buoyancy = 0.5
upwind_table = ((1.0, 1.0), (-8.0, -5.0), (37.0, 10.0), (37.0, -10.0), (-8.0, 5.0), (1.0, -1.0))

def take_part(array, start, count, axis):
    return lax.slice_in_dim(array, start, start + count, axis=axis)

def pad_three(field, axis):
    widths = [(0, 0)] * field.ndim
    widths[axis] = (3, 3)
    return jnp.pad(field, widths)

def forward_tend(padded, wind_pad, axis):
    count = padded.shape[axis] - 6
    speed = take_part(wind_pad, 2, count + 1, axis)
    magnitude = jnp.abs(speed)
    flux = jnp.zeros_like(speed)
    for offset, pair in enumerate(upwind_table):
        flux = flux + (pair[0] * speed + pair[1] * magnitude) / 60.0 * take_part(padded, offset, count + 1, axis)
    return -courant * (take_part(flux, 1, count, axis) - take_part(flux, 0, count, axis))

def adjoint_tend(padded, wind_pad, axis):
    count = padded.shape[axis] - 6
    face_bar = courant * (take_part(padded, 1, count + 5, axis) - take_part(padded, 0, count + 5, axis))
    speed = take_part(wind_pad, 0, count + 5, axis)
    magnitude = jnp.abs(speed)
    result = jnp.zeros_like(take_part(padded, 3, count, axis))
    for offset, pair in enumerate(upwind_table):
        weighted = (pair[0] * speed + pair[1] * magnitude) / 60.0 * face_bar
        result = result + take_part(weighted, 5 - offset, count, axis)
    return result

def level_forward(items):
    field, east, north = items
    return forward_tend(pad_three(field, 0), pad_three(east, 0), 0) + forward_tend(pad_three(field, 1), pad_three(north, 1), 1)

def level_adjoint(items):
    field, east, north = items
    return adjoint_tend(pad_three(field, 0), pad_three(east, 0), 0) + adjoint_tend(pad_three(field, 1), pad_three(north, 1), 1)

def laplace(field):
    padded = jnp.pad(field, ((0, 0), (1, 1), (1, 1)))
    return padded[:, 2:, 1:-1] + padded[:, :-2, 1:-1] + padded[:, 1:-1, 2:] + padded[:, 1:-1, :-2] - 4.0 * field

def solve_transposed(field, sound_coef):
    levels, rows, columns = field.shape
    zero_one = jnp.zeros((1,), sound_coef.dtype)
    lower = jnp.concatenate([zero_one, -sound_coef[:-1]])
    upper = jnp.concatenate([-sound_coef[1:], zero_one])
    middle = 1.0 + 2.0 * sound_coef
    flat = field.reshape(levels, rows * columns)
    solved = lax.linalg.tridiagonal_solve(lower, middle, upper, flat)
    return solved.reshape(levels, rows, columns)

def reference(theta, winds, theta_bar, press_bar, urban_frac, wall_temp, urban_class, canopy_layers, height_bin, class_drag, bin_profile, sound_coef):
    drag_col = class_drag[urban_class]
    profile = jnp.transpose(bin_profile[height_bin], (2, 0, 1))
    levels = jnp.arange(theta.shape[0], dtype=jnp.int32)[:, None, None]
    active = (levels < canopy_layers[None]).astype(theta.dtype)
    amount = urban_frac[None] * drag_col[None] * profile * active
    first = theta + lax.map(level_forward, (theta, winds[0], winds[1]))
    press_back = press_bar
    stacked_q = jnp.zeros_like(theta)
    for substep in range(2):
        solved = solve_transposed(press_back, sound_coef)
        stacked_q = stacked_q + solved
        press_back = solved + diffusion * laplace(solved)
    press_grad = press_back
    second_bar = theta_bar + buoyancy * stacked_q
    first_bar = (1.0 - amount) * second_bar
    theta_grad = first_bar + lax.map(level_adjoint, (first_bar, winds[0], winds[1]))
    frac_grad = jnp.sum(drag_col[None] * profile * active * (wall_temp[None] - first) * second_bar, axis=0)
    wall_grad = jnp.sum(amount * second_bar, axis=0)
    return (theta_grad, press_grad, frac_grad, wall_grad)
```

```python
import jax
import jax.numpy as jnp
from jax import lax
from jax.sharding import PartitionSpec as P

courant = 0.3
diffusion = 0.1
buoyancy = 0.5
upwind_table = ((1.0, 1.0), (-8.0, -5.0), (37.0, 10.0), (37.0, -10.0), (-8.0, 5.0), (1.0, -1.0))


def padded_2(shard, sides, width):
    for axis, dim in sides:
        peers, length = (lax.axis_size(axis), shard.shape[dim])
        up = [(i, (i + 1) % peers) for i in range(peers - 1)]
        down = [(j, i) for i, j in up]
        last = lax.slice_in_dim(shard, length - width, length, axis=dim)
        leading = lax.slice_in_dim(shard, 0, width, axis=dim)
        before = lax.ppermute(last, axis, up)
        after = lax.ppermute(leading, axis, down)
        shard = jnp.concatenate([before, shard, after], axis=dim)
    return shard


def take_part(array, start, count, axis):
    return lax.slice_in_dim(array, start, start + count, axis=axis)


def forward_tend(padded, wind_pad, axis):
    count = padded.shape[axis] - 6
    speed = take_part(wind_pad, 2, count + 1, axis)
    magnitude = jnp.abs(speed)
    flux = jnp.zeros_like(speed)
    for offset, pair in enumerate(upwind_table):
        flux = flux + (pair[0] * speed + pair[1] * magnitude) / 60.0 * take_part(
            padded, offset, count + 1, axis
        )
    return -courant * (take_part(flux, 1, count, axis) - take_part(flux, 0, count, axis))


def adjoint_tend(padded, wind_pad, axis):
    count = padded.shape[axis] - 6
    face_bar = courant * (
        take_part(padded, 1, count + 5, axis) - take_part(padded, 0, count + 5, axis)
    )
    speed = take_part(wind_pad, 0, count + 5, axis)
    magnitude = jnp.abs(speed)
    result = jnp.zeros(take_part(padded, 3, count, axis).shape, jnp.float32)
    for offset, pair in enumerate(upwind_table):
        weighted = (pair[0] * speed + pair[1] * magnitude) / 60.0 * face_bar
        result = result + take_part(weighted, 5 - offset, count, axis)
    return result


def laplace(extended):
    return (
        extended[:, 2:, 1:-1]
        + extended[:, :-2, 1:-1]
        + extended[:, 1:-1, 2:]
        + extended[:, 1:-1, :-2]
        - 4.0 * extended[:, 1:-1, 1:-1]
    )


def transposed_inverse(sound_coef):
    levels = sound_coef.shape[0]
    size = 1
    while size < levels:
        size *= 2
    padding = jnp.zeros((size - levels,), jnp.float32)
    lower = jnp.concatenate([jnp.zeros((1,), jnp.float32), -sound_coef[:-1], padding])
    upper = jnp.concatenate([-sound_coef[1:], jnp.zeros((1,), jnp.float32), padding])
    middle = jnp.concatenate([1.0 + 2.0 * sound_coef, padding + 1.0])
    blocks = (1.0 / middle).reshape(size, 1, 1)
    width = 1
    while width < size:
        first, second = blocks[0::2], blocks[1::2]
        up = upper[width - 1 :: 2 * width][:, None, None]
        low = lower[width :: 2 * width][:, None, None]
        tail_col, tail_row = first[:, :, -1:], first[:, -1:, :]
        head_col, head_row = second[:, :, :1], second[:, :1, :]
        corner, head = first[:, -1:, -1:], second[:, :1, :1]
        scale = 1.0 / (1.0 - up * low * corner * head)
        blocks = jnp.concatenate(
            [
                jnp.concatenate(
                    [
                        first + tail_col * (up * low * head * scale) * tail_row,
                        -tail_col * (up * scale) * head_row,
                    ],
                    axis=2,
                ),
                jnp.concatenate(
                    [
                        -head_col * (low * scale) * tail_row,
                        second + head_col * (up * low * corner * scale) * head_row,
                    ],
                    axis=2,
                ),
            ],
            axis=1,
        )
        width *= 2
    return blocks[0, :levels, :levels]


def solve_transposed(field, inverse):
    return lax.dot_general(
        inverse, field, (((1,), (0,)), ((), ())), precision=lax.Precision.HIGHEST
    )


def per_device(
    theta,
    winds,
    theta_bar,
    press_bar,
    urban_frac,
    wall_temp,
    urban_class,
    canopy_layers,
    height_bin,
    class_drag,
    bin_profile,
    sound_coef,
):
    levels, rows, columns = theta.shape
    canopy = min(levels, 8)
    classes = class_drag.shape[0]
    bins = bin_profile.shape[0]
    class_hot = (urban_class[None] == jnp.arange(classes, dtype=jnp.int32)[:, None, None]).astype(
        jnp.float32
    )
    drag_col = jnp.sum(class_hot * class_drag[:, None, None], axis=0)
    bin_hot = (
        height_bin.reshape(1, rows * columns) == jnp.arange(bins, dtype=jnp.int32)[:, None]
    ).astype(jnp.float32)
    profile = jnp.dot(bin_profile[:, :canopy].T, bin_hot, precision=lax.Precision.HIGHEST).reshape(
        canopy, rows, columns
    )
    level_ids = jnp.arange(canopy, dtype=jnp.int32)[:, None, None]
    active = (level_ids < canopy_layers[None]).astype(jnp.float32)
    amount = urban_frac[None] * drag_col[None] * profile * active
    keeping = 1.0 - amount
    wind_east = padded_2(winds[0], (("gx", 1),), 3)
    wind_north = padded_2(winds[1], (("gy", 2),), 3)
    low_theta = theta[:canopy]
    theta_east = padded_2(low_theta, (("gx", 1),), 3)
    theta_north = padded_2(low_theta, (("gy", 2),), 3)
    first = (
        low_theta
        + forward_tend(theta_east, wind_east[:canopy], 1)
        + forward_tend(theta_north, wind_north[:canopy], 2)
    )
    inverse = transposed_inverse(sound_coef)
    press_back = press_bar
    stacked_q = jnp.zeros_like(theta)
    for substep in range(2):
        solved = solve_transposed(press_back, inverse)
        stacked_q = stacked_q + solved
        solved_ext = padded_2(solved, (("gx", 1), ("gy", 2)), 1)
        press_back = solved + diffusion * laplace(solved_ext)
    second_bar = theta_bar + buoyancy * stacked_q
    low_bar = second_bar[:canopy]
    first_bar = jnp.concatenate([keeping * low_bar, second_bar[canopy:]], axis=0)
    first_east = padded_2(first_bar, (("gx", 1),), 3)
    first_north = padded_2(first_bar, (("gy", 2),), 3)
    theta_grad = (
        first_bar
        + adjoint_tend(first_east, wind_east, 1)
        + adjoint_tend(first_north, wind_north, 2)
    )
    frac_grad = jnp.sum(
        drag_col[None] * profile * active * (wall_temp[None] - first) * low_bar, axis=0
    )
    wall_grad = jnp.sum(amount * low_bar, axis=0)
    return (theta_grad, press_back, frac_grad, wall_grad)


def solution(mesh):
    in_specs = (
        P(None, "gx", "gy"),
        P(None, None, "gx", "gy"),
        P(None, "gx", "gy"),
        P(None, "gx", "gy"),
        P("gx", "gy"),
        P("gx", "gy"),
        P("gx", "gy"),
        P("gx", "gy"),
        P("gx", "gy"),
        P(),
        P(),
        P(),
    )
    out_specs = (P(None, "gx", "gy"), P(None, "gx", "gy"), P("gx", "gy"), P("gx", "gy"))
    return jax.shard_map(
        per_device, mesh=mesh, in_specs=in_specs, out_specs=out_specs, check_vma=False
    )
```
